32 devices in a mesh: req: 8 (over z, x), tp: 4 (over y, core).
Axes of the slice: x: 2, y: 2, z: 4, core: 2. Of those that a mesh axis runs over, the one named last changes fastest.
Arguments:
- tokens: bfloat16 [4096, 1408], P('req', 'tp'), may hold values from -24 to 24
- ln1_gain: float32 [1408], replicated, may hold values from 0.1 to 1.9
- ln1_bias: float32 [1408], replicated, may hold values from -3 to 3
- qkv_weight: bfloat16 [3, 1408, 1408], P(None, None, 'tp'), may hold values from -6 to 6
- out_weight: bfloat16 [1408, 1408], P('tp'), may hold values from -0.15625 to 0.15625
- ln2_gain: float32 [1408], replicated, may hold values from 0.25 to 1.75
- ln2_bias: float32 [1408], replicated, may hold values from -3 to 3
- merger_weight: bfloat16 [5632, 3584], P('req', 'tp'), may hold values from -0.078125 to 0.078125
- group_segments: int32 [8, 128], P('req'), may hold values from 0 to 7, never falling along the last dimension, each value on 1 to 41 neighbouring positions
- owners: int32 [1024, 1], P('req'), may hold values from 0 to 7; in each aligned block of 128 rows (0 to 127, 128 to 255, ...) at most 32 rows name the same one
Outputs:
- received: bfloat16 [2048, 3584], P('req', 'tp')
The draws below stay inside these ranges and needn't reach their ends.
Inputs may be any that keep to these rules, and one draw needn't show every extreme that they name: `group_segments`: never falling along a request's groups; every picture has 1 to 41 groups and one has exactly 41. `owners`: among the 128 groups of one request no owner appears more than 32 times; in every draw some request sends exactly 32 to some owner.
All inputs are finite; a program needn't handle non-finite values.
Results may differ from the reference program's by a relative error of at most 0.009.
Values may be sent and summed in bfloat16 or wider, within the bound.
A program may use at most 128 MiB of HBM per device.

```python
import math
import jax
import jax.numpy as jnp
import numpy as np
from jax import lax

D = 1408
HEADS = 16
HEAD_DIM = 88
OUT = 3584
MERGE_DEV = 128
PICS = 8
TOK_DEV = 512
GMOST = 41
TOKENS = 4096
MERGED = 1024
CAP = 32
N_REQ = 8


def draw_tokens(key, part):
    key_base, key_cols, key_rows = jax.random.split(key, 3)
    ramp = 3.0 ** (jnp.arange(D, dtype=jnp.float32) / (D - 1))
    col_scale = ramp * jnp.exp(jax.random.uniform(key_cols, (D,), jnp.float32, math.log(0.3), math.log(3.0)))
    row_scale = jnp.exp(jax.random.uniform(key_rows, (TOKENS, 1), jnp.float32, math.log(0.3), math.log(3.0)))
    values = jax.random.normal(key_base, (TOKENS, D), jnp.float32) * row_scale * col_scale
    return jnp.clip(values, -24.0, 24.0).astype(jnp.bfloat16)


def draw_qkv_weight(key, part):
    key_base = jax.random.fold_in(key, 0)
    base = jax.random.normal(key_base, (3, D, D), jnp.float32) / math.sqrt(D)
    values = base
    return jnp.clip(values, -6.0, 6.0).astype(jnp.bfloat16)


def block_scale(own_key, shape, cuts, low, high):
    loudness, own = 1.0, jax.random.fold_in(own_key, 6)
    for axis_at, shards_of in cuts:
        heights = jnp.exp(jax.random.uniform(jax.random.fold_in(own, axis_at), (shards_of,), jnp.float32, low / len(cuts), high / len(cuts)))
        loudness = loudness * jnp.repeat(heights, shape[axis_at] // shards_of).reshape([-1 if axis == axis_at else 1 for axis in range(len(shape))])
    return loudness


def profile(amount, total, most, lean):
    loads = [(1 << 20) // math.isqrt(grade ** lean) + 1 for grade in range(2, amount + 1)]
    rest, counts = total - most - (amount - 1), [1] * (amount - 1)
    while rest > 0:
        candidates = [i for i in range(amount - 1) if counts[i] < most]
        mass, budget = sum([loads[i] for i in candidates]), rest
        for i in candidates:
            more = min(most - counts[i], max(1, budget * loads[i] // mass), rest)
            counts[i] = counts[i] + more
            rest = rest - more
    return np.array([most] + counts)


def uneven(rng, count, total, most, skew):
    if count == 2:
        one = jax.random.randint(rng, (), max(1, total - most), min(most, total - 1) + 1)
        return jnp.stack([one, total - one])
    sizes = jnp.asarray(profile(count, total, most, skew), jnp.int32)
    twos = (count - 1) // 2
    giver, receiver = sizes[1:1 + 2 * twos:2], sizes[2:2 + 2 * twos:2]
    slack = jnp.minimum(giver - 1, most - receiver)
    moved = jax.random.randint(jax.random.fold_in(rng, 1), (twos,), 0, 1 << 20) % (slack + 1)
    sizes = sizes.at[1:1 + 2 * twos:2].set(giver - moved).at[2:2 + 2 * twos:2].set(receiver + moved)
    return sizes[jax.random.permutation(jax.random.fold_in(rng, 2), count)]


def assign_block(stream_key, own, number, rows, amount, top, bound, slope):
    sequence = jax.random.permutation(stream_key, amount)
    packed, ordinary = shares(amount, rows * top, bound, slope, True), shares(amount, rows * top, bound, slope, False)
    places = jnp.arange(amount)

    def named(tallies, offset_by):
        used = int((tallies > 0).sum())
        fixed = max(1, used // 4)
        moved = fixed + (places - fixed + offset_by * (used - fixed)) % max(1, amount - fixed)
        return jnp.zeros((amount,), jnp.int32).at[sequence[jnp.where(places < fixed, places, moved)]].set(jnp.asarray(tallies, jnp.int32))

    tallies = jnp.where(number % 4 == 0, named(packed, number // 4), named(ordinary, number - number // 4 - 1))
    mixed = jax.random.permutation(jax.random.fold_in(own, 3), amount)
    donor, taker = mixed[0:amount // 2 * 2:2], mixed[1:amount // 2 * 2:2]
    room = jnp.minimum(tallies[donor] - 1, bound - tallies[taker]) // 2
    room = jnp.where((donor == sequence[0]) | (taker == sequence[0]) | (tallies[taker] == 0), 0, jnp.maximum(room, 0))
    moved = jax.random.randint(jax.random.fold_in(own, 4), (amount // 2,), 0, 1 << 20) % (room + 1)
    tallies = tallies.at[donor].add(-moved).at[taker].add(moved)
    members = jnp.searchsorted(jnp.cumsum(tallies), jnp.arange(rows * top), side="right").astype(jnp.int32)
    grid = members.reshape(top, rows).T
    grid = grid[jax.random.permutation(jax.random.fold_in(own, 1), rows)]
    offset_by = jax.random.randint(jax.random.fold_in(own, 2), (rows, 1), 0, top)
    return jnp.take_along_axis(grid, (jnp.arange(top)[None, :] + offset_by) % top, axis=1)


def shares(amount, total, bound, skew, full):
    loads = [(1 << 20) // math.isqrt(grade ** skew) + 1 for grade in range(1, amount + 1)]
    largest = bound if full else min(bound, max(-(-total // amount), total * loads[0] // sum(loads)))
    least = 1 if total - largest >= amount - 1 else 0
    counts, spare = [largest] + [least] * (amount - 1), total - largest - least * (amount - 1)
    while spare > 0:
        movable = [i for i in range(1, amount) if counts[i] < largest] or [i for i in range(1, amount) if counts[i] < bound]
        mass, remaining = sum([loads[i] for i in movable]), spare
        for i in movable:
            extra = min(bound - counts[i], max(1, remaining * loads[i] // mass), spare)
            counts[i] = counts[i] + extra
            spare = spare - extra
    return np.array(counts)


def bell_draw(own_key, shape, spread, reach, shards=(), kind=jnp.bfloat16):
    factor_of = block_scale(own_key, shape, shards, -0.22, 0.18) if shards else 1.0
    entries = jax.random.normal(own_key, shape, jnp.float32) * spread * factor_of
    return jnp.minimum(jnp.maximum(entries, -reach), reach).astype(kind)


def setup_inputs(seed: int = 0) -> dict:
    streams_of = jax.random.split(jax.random.key(seed), 11)
    tokens = draw_tokens(jax.random.fold_in(streams_of[10], 71), 0)
    ln1_gain = jnp.clip(1.0 + 0.18 * jax.random.normal(streams_of[1], (D,), jnp.float32), 0.1, 1.9)
    ln1_bias = bell_draw(streams_of[2], (D,), 0.5, 3.0, (), jnp.float32)
    qkv_weight = draw_qkv_weight(jax.random.fold_in(streams_of[10], 71), 0)
    out_weight = bell_draw(streams_of[4], (D, D), D ** -0.5, 0.15625, ((0, 4),))
    ln2_gain = jnp.clip(1.0 + 0.15 * jax.random.normal(streams_of[5], (D,), jnp.float32), 0.25, 1.75)
    ln2_bias = bell_draw(streams_of[6], (D,), 0.5, 3.0, (), jnp.float32)
    merger_weight = bell_draw(streams_of[7], (4 * D, OUT), (4 * D) ** -0.5, 0.078125, ((0, 8), (1, 4)))
    group_segments = jax.vmap(lambda own: jnp.searchsorted(jnp.cumsum(uneven(own, PICS, MERGE_DEV, GMOST, 2)), jnp.arange(MERGE_DEV), side="right"))(jax.random.split(streams_of[8], N_REQ)).reshape((N_REQ, MERGE_DEV)).astype(jnp.int32)
    owners_keys = jax.random.split(jax.random.fold_in(streams_of[9], 1), MERGED // MERGE_DEV)
    owners_turns = jax.random.permutation(jax.random.fold_in(streams_of[9], 3), MERGED // MERGE_DEV)
    owners = jax.vmap(lambda own, number: assign_block(jax.random.fold_in(streams_of[9], 2), own, number, MERGE_DEV, N_REQ, 1, CAP, 2))(owners_keys, owners_turns).reshape((MERGED, 1))
    return {"tokens": tokens, "ln1_gain": ln1_gain, "ln1_bias": ln1_bias, "qkv_weight": qkv_weight, "out_weight": out_weight, "ln2_gain": ln2_gain, "ln2_bias": ln2_bias, "merger_weight": merger_weight, "group_segments": group_segments, "owners": owners}


epsilon = 1e-06

def layer_norm(values, gain, bias):
    row_mean = lax.optimization_barrier(jnp.mean(values, axis=-1, keepdims=True))
    shifted = values - row_mean
    variance = lax.optimization_barrier(jnp.mean(shifted * shifted, axis=-1, keepdims=True))
    return shifted * lax.rsqrt(variance + epsilon) * gain + bias

def reference(tokens, ln1_gain, ln1_bias, qkv_weight, out_weight, ln2_gain, ln2_bias, merger_weight, group_segments, owners):
    qkv_float = qkv_weight.astype(jnp.float32)

    def encode(inputs):
        block, segment_row = inputs
        normed = layer_norm(block.astype(jnp.float32), ln1_gain, ln1_bias).astype(jnp.bfloat16)
        combined = jnp.einsum('td,cdh->cth', normed.astype(jnp.float32), qkv_float, precision=lax.Precision.HIGHEST)
        combined = combined.astype(jnp.bfloat16).astype(jnp.float32).reshape(3, TOK_DEV, HEADS, HEAD_DIM)
        scores = jnp.einsum('qhd,khd->hqk', combined[0], combined[1], precision=lax.Precision.HIGHEST) * HEAD_DIM ** (-0.5)
        segment_ids = jnp.repeat(segment_row, 4)
        same_picture = segment_ids[:, None] == segment_ids[None, :]
        scores = jnp.where(same_picture[None], scores, -1e+30)
        row_max = lax.optimization_barrier(jnp.max(scores, axis=2, keepdims=True))
        exponent = jnp.exp(scores - row_max)
        weights = (exponent / lax.optimization_barrier(jnp.sum(exponent, axis=2, keepdims=True))).astype(jnp.bfloat16)
        context = jnp.einsum('hqk,khd->qhd', weights.astype(jnp.float32), combined[2], precision=lax.Precision.HIGHEST)
        context = context.astype(jnp.bfloat16).reshape(TOK_DEV, D)
        hidden = block.astype(jnp.float32) + jnp.dot(context, out_weight, preferred_element_type=jnp.float32)
        patches = layer_norm(hidden, ln2_gain, ln2_bias).astype(jnp.bfloat16)
        flat = patches.reshape(MERGE_DEV, 4 * D)
        return jnp.dot(flat, merger_weight, preferred_element_type=jnp.float32).astype(jnp.bfloat16)
    projected = lax.map(encode, (tokens.reshape(N_REQ, TOK_DEV, D), group_segments))
    target = owners[:, 0].astype(jnp.int32).reshape(N_REQ, MERGE_DEV)
    owner_ids = jnp.arange(N_REQ).astype(jnp.int32)
    owner_hits = (target[:, :, None] == owner_ids[None, None, :]).astype(jnp.int32)
    before = (jnp.cumsum(owner_hits, axis=1).astype(jnp.int32) - owner_hits).astype(jnp.int32)
    slot_rank = lax.optimization_barrier(jnp.sum(before * owner_hits, axis=2)).astype(jnp.int32)
    destination = ((target * N_REQ + owner_ids[:, None]) * CAP + slot_rank).astype(jnp.int32).reshape(-1)
    received = jnp.zeros((N_REQ * N_REQ * CAP, OUT), jnp.bfloat16)
    return received.at[destination].set(projected.reshape(N_REQ * MERGE_DEV, OUT))
```

```python
import jax
import jax.numpy as jnp
from jax import lax
from jax.sharding import PartitionSpec as P

HEAD_DIM = 88


epsilon = 1e-06


def layer_norm(values, gain, bias):
    mean = jnp.mean(values, axis=1, keepdims=True)
    centered = values - mean
    variance = jnp.mean(centered * centered, axis=1, keepdims=True)
    return (centered * lax.rsqrt(variance + epsilon) * gain + bias).astype(jnp.bfloat16)


def local(
    tokens,
    ln1_gain,
    ln1_bias,
    qkv_weight,
    out_weight,
    ln2_gain,
    ln2_bias,
    merger_weight,
    group_segments,
    owners,
):
    tp_count = lax.axis_size("tp")
    req_count = lax.axis_size("req")
    tp_index = lax.axis_index("tp")
    req_index = lax.axis_index("req")
    half = req_count // 2
    upper = req_index // half
    tok_count = tokens.shape[0]
    width = tokens.shape[1] * tp_count
    row_count = tok_count // tp_count
    group_count = tok_count // 4
    own_groups = group_count // tp_count
    out_cols = merger_weight.shape[1]
    gathered = lax.all_gather(tokens, "tp", axis=1, tiled=True)
    gathered, merger_part = lax.optimization_barrier((gathered, merger_weight))
    halves = [list(range(half)), list(range(half, req_count))]
    kept_weight = lax.all_gather(
        merger_part, "req", axis=0, tiled=True, axis_index_groups=halves
    )
    normed = layer_norm(gathered.astype(jnp.float32), ln1_gain, ln1_bias)
    combined = jnp.einsum("td,cdh->cth", normed, qkv_weight, preferred_element_type=jnp.float32)
    combined = combined.astype(jnp.bfloat16).reshape(3, tok_count, -1, HEAD_DIM)
    queries, key_heads, value_heads = (combined[0], combined[1], combined[2])
    segment_ids = jnp.repeat(group_segments[0], 4)
    same_picture = segment_ids[:, None] == segment_ids[None, :]
    scores = jnp.einsum(
        "qhd,khd->hqk", queries, key_heads, preferred_element_type=jnp.float32
    ) * HEAD_DIM ** (-0.5)
    scores = jnp.where(same_picture[None], scores, -1e30)
    row_max = jnp.max(scores, axis=2, keepdims=True)
    exponent = jnp.exp(scores - row_max)
    weights = (exponent / jnp.sum(exponent, axis=2, keepdims=True)).astype(jnp.bfloat16)
    context = jnp.einsum("hqk,khd->qhd", weights, value_heads, preferred_element_type=jnp.float32)
    context = context.astype(jnp.bfloat16).reshape(tok_count, -1)
    partial_value = jnp.dot(context, out_weight, preferred_element_type=jnp.float32)
    pieces = partial_value.astype(jnp.bfloat16).reshape(tp_count, row_count, width)

    def rows_of(array, index):
        return lax.dynamic_index_in_dim(array, index, 0, keepdims=False)

    hidden = rows_of(gathered.reshape(tp_count, row_count, width), tp_index).astype(jnp.float32)
    hidden += rows_of(partial_value.reshape(tp_count, row_count, width), tp_index)
    for step in range(1, tp_count):
        leaving = rows_of(pieces, (tp_index + step) % tp_count)
        hidden += lax.ppermute(
            leaving, "tp", [(i, (i + step) % tp_count) for i in range(tp_count)]
        ).astype(jnp.float32)
    patches = layer_norm(hidden, ln2_gain, ln2_bias)
    merged = patches.reshape(own_groups, 2, 2 * width)
    swap = [(i, (i + half) % req_count) for i in range(req_count)]
    staying = lax.dynamic_index_in_dim(merged, upper, 1, keepdims=False)
    going = lax.dynamic_index_in_dim(merged, 1 - upper, 1, keepdims=False)
    coming = lax.ppermute(going, "req", swap)
    both = jnp.stack([staying, coming])
    full = lax.all_gather(both, "tp", axis=1, tiled=True)
    projected = jnp.dot(
        full.reshape(2 * group_count, 2 * width),
        kept_weight,
        preferred_element_type=jnp.float32,
    )
    arriving = lax.ppermute(projected[group_count:].astype(jnp.bfloat16), "req", swap)
    projected = projected[:group_count] + arriving.astype(jnp.float32)
    projected = projected.astype(jnp.bfloat16)
    capacity = max(2, 2 * group_count // req_count)
    slot_count = req_count * capacity
    target = owners[:, 0]
    same_owner = target[:, None] == target[None, :]
    place = jnp.arange(group_count, dtype=jnp.int32)
    earlier = same_owner & (place[None, :] < place[:, None])
    slot_rank = jnp.sum(earlier.astype(jnp.int32), axis=1)
    slot_index = target * capacity + slot_rank
    placing = (slot_index[None, :] == jnp.arange(slot_count, dtype=jnp.int32)[:, None]).astype(
        jnp.bfloat16
    )
    outgoing = jnp.dot(placing, projected, preferred_element_type=jnp.float32).astype(jnp.bfloat16)
    outgoing = outgoing.reshape(req_count, capacity, out_cols)
    arrived = lax.all_to_all(outgoing, "req", split_axis=0, concat_axis=0, tiled=True)
    return arrived.reshape(slot_count, out_cols)


def solution(mesh):
    in_specs = (
        P("req", "tp"),
        P(),
        P(),
        P(None, None, "tp"),
        P("tp", None),
        P(),
        P(),
        P("req", "tp"),
        P("req", None),
        P("req", None),
    )
    out_specs = P("req", "tp")
    return jax.shard_map(local, mesh=mesh, in_specs=in_specs, out_specs=out_specs, check_vma=False)
```

```python
import jax
import jax.numpy as jnp
from jax import lax
from jax.experimental import pallas as pl
from jax.experimental.pallas import tpu as pltpu
from jax.sharding import PartitionSpec as P

HEAD_DIM = 88


epsilon = 1e-06


def layer_norm(values, gain, bias):
    mean = jnp.mean(values, axis=1, keepdims=True)
    centered = values - mean
    variance = jnp.mean(centered * centered, axis=1, keepdims=True)
    return (centered * lax.rsqrt(variance + epsilon) * gain + bias).astype(jnp.bfloat16)


def local(
    tokens,
    ln1_gain,
    ln1_bias,
    qkv_weight,
    out_weight,
    ln2_gain,
    ln2_bias,
    merger_weight,
    group_segments,
    owners,
):
    tp_count = lax.axis_size("tp")
    req_count = lax.axis_size("req")
    tp_index = lax.axis_index("tp")
    req_index = lax.axis_index("req")
    half = req_count // 2
    upper = req_index // half
    tok_count = tokens.shape[0]
    width = tokens.shape[1] * tp_count
    row_count = tok_count // tp_count
    group_count = tok_count // 4
    own_groups = group_count // tp_count
    out_cols = merger_weight.shape[1]
    gathered = lax.all_gather(tokens, "tp", axis=1, tiled=True)
    gathered, merger_part = lax.optimization_barrier((gathered, merger_weight))
    halves = [list(range(half)), list(range(half, req_count))]
    kept_weight = lax.all_gather(
        merger_part, "req", axis=0, tiled=True, axis_index_groups=halves
    )
    normed = layer_norm(gathered.astype(jnp.float32), ln1_gain, ln1_bias)
    combined = jnp.einsum("td,cdh->cth", normed, qkv_weight, preferred_element_type=jnp.float32)
    combined = combined.astype(jnp.bfloat16).reshape(3, tok_count, -1, HEAD_DIM)
    queries, key_heads, value_heads = (combined[0], combined[1], combined[2])
    segment_ids = jnp.repeat(group_segments[0], 4)
    same_picture = segment_ids[:, None] == segment_ids[None, :]
    scores = jnp.einsum(
        "qhd,khd->hqk", queries, key_heads, preferred_element_type=jnp.float32
    ) * HEAD_DIM ** (-0.5)
    scores = jnp.where(same_picture[None], scores, -1e30)
    row_max = jnp.max(scores, axis=2, keepdims=True)
    exponent = jnp.exp(scores - row_max)
    weights = (exponent / jnp.sum(exponent, axis=2, keepdims=True)).astype(jnp.bfloat16)
    context = jnp.einsum("hqk,khd->qhd", weights, value_heads, preferred_element_type=jnp.float32)
    context = context.astype(jnp.bfloat16).reshape(tok_count, -1)
    partial_value = jnp.dot(context, out_weight, preferred_element_type=jnp.float32)
    pieces = partial_value.astype(jnp.bfloat16).reshape(tp_count, row_count, width)

    def rows_of(array, index):
        return lax.dynamic_index_in_dim(array, index, 0, keepdims=False)

    hidden = rows_of(gathered.reshape(tp_count, row_count, width), tp_index).astype(jnp.float32)
    hidden += rows_of(partial_value.reshape(tp_count, row_count, width), tp_index)
    for step in range(1, tp_count):
        leaving = rows_of(pieces, (tp_index + step) % tp_count)
        hidden += lax.ppermute(
            leaving, "tp", [(i, (i + step) % tp_count) for i in range(tp_count)]
        ).astype(jnp.float32)
    patches = layer_norm(hidden, ln2_gain, ln2_bias)
    merged = patches.reshape(own_groups, 2, 2 * width)
    swap = [(i, (i + half) % req_count) for i in range(req_count)]
    staying = lax.dynamic_index_in_dim(merged, upper, 1, keepdims=False)
    going = lax.dynamic_index_in_dim(merged, 1 - upper, 1, keepdims=False)
    coming = lax.ppermute(going, "req", swap)
    both = jnp.stack([staying, coming])
    full = lax.all_gather(both, "tp", axis=1, tiled=True)
    projected = jnp.dot(
        full.reshape(2 * group_count, 2 * width),
        kept_weight,
        preferred_element_type=jnp.float32,
    )
    arriving = lax.ppermute(projected[group_count:].astype(jnp.bfloat16), "req", swap)
    projected = projected[:group_count] + arriving.astype(jnp.float32)
    projected = projected.astype(jnp.bfloat16)
    capacity = max(2, 2 * group_count // req_count)
    slot_count = req_count * capacity
    target = owners[:, 0]
    same_owner = target[:, None] == target[None, :]
    place = jnp.arange(group_count, dtype=jnp.int32)
    earlier = same_owner & (place[None, :] < place[:, None])
    slot_rank = jnp.sum(earlier.astype(jnp.int32), axis=1)
    slot_index = target * capacity + slot_rank
    placing = (slot_index[None, :] == jnp.arange(slot_count, dtype=jnp.int32)[:, None]).astype(
        jnp.bfloat16
    )
    outgoing = jnp.dot(placing, projected, preferred_element_type=jnp.float32).astype(jnp.bfloat16)
    outgoing = outgoing.reshape(req_count, capacity, out_cols)
    arrived = lax.all_to_all(outgoing, "req", split_axis=0, concat_axis=0, tiled=True)
    return arrived.reshape(slot_count, out_cols)


def dot(left, right, contract):
    return lax.dot_general(
        left, right, ((contract[:1], contract[1:]), ((), ())), preferred_element_type=jnp.float32
    )


def kernel(
    tokens_ref,
    gain1_ref,
    bias1_ref,
    qkv_ref,
    out_weight_ref,
    gain2_ref,
    bias2_ref,
    merger_ref,
    seg_col_ref,
    seg_row_ref,
    own_col_ref,
    own_row_ref,
    result_ref,
    gath,
    normed,
    heads,
    leaving,
    landing,
    own_sum,
    merged,
    going,
    held,
    half_out,
    half_in,
    outgoing,
    local_sem,
    send_sem,
    recv_sem,
):
    tp = lax.axis_index("tp")
    req = lax.axis_index("req")
    feats, tok_count = tokens_ref.shape
    full = gath.shape[0]
    rows = tok_count // 4
    groups = tok_count // 4
    part = rows // 4
    shard = merger_ref.shape[0]
    cut = shard // 2
    place = req % 4
    upper = req // 4
    across = (req + 4) % 8
    beside = req + 1 - 2 * (req % 2)
    above = req - place + (place + 2) % 4
    capacity = result_ref.shape[0] // 8

    def remote(source, target, index, device):
        return pltpu.make_async_remote_copy(
            src_ref=source,
            dst_ref=target,
            send_sem=send_sem.at[index],
            recv_sem=recv_sem.at[index],
            device_id=device,
            device_id_type=pl.DeviceIdType.MESH,
        )

    barrier = pltpu.get_barrier_semaphore()
    for step in range(1, 4):
        pl.semaphore_signal(
            barrier, inc=1, device_id=(req, (tp + step) % 4), device_id_type=pl.DeviceIdType.MESH
        )
    for step in range(1, 8):
        pl.semaphore_signal(
            barrier, inc=1, device_id=((req + step) % 8, tp), device_id_type=pl.DeviceIdType.MESH
        )
    pl.semaphore_wait(barrier, 10)

    mine = pl.ds(pl.multiple_of(tp * feats, 16), feats)
    token_copies = [
        remote(tokens_ref, gath.at[mine], step - 1, (req, (tp + step) % 4)) for step in range(1, 4)
    ]
    for copy in token_copies:
        copy.start()

    def weight_rows(owner, lower):
        return pl.ds(pl.multiple_of(owner * shard + lower * cut, 16), cut)

    first, second = merger_ref.at[pl.ds(0, cut)], merger_ref.at[pl.ds(cut, cut)]
    to_beside = [
        remote(first, held.at[weight_rows(place, 0)], 3, (beside, tp)),
        remote(second, held.at[weight_rows(place, 1)], 4, (beside, tp)),
    ]
    to_above = [
        remote(second, held.at[weight_rows(place, 1)], 5, (above, tp)),
        remote(first, held.at[weight_rows(place, 0)], 6, (above, tp)),
    ]
    to_beside[0].start()
    to_above[0].start()
    to_beside[1].start()
    to_above[1].start()
    own_weight = pltpu.make_async_copy(
        merger_ref, held.at[pl.ds(pl.multiple_of(place * shard, 16), shard)], local_sem
    )
    own_weight.start()
    beside_place, above_place = beside % 4, above % 4
    relay_above = remote(
        held.at[weight_rows(beside_place, 0)],
        held.at[weight_rows(beside_place, 0)],
        7,
        (above, tp),
    )
    relay_beside = remote(
        held.at[weight_rows(above_place, 1)],
        held.at[weight_rows(above_place, 1)],
        8,
        (beside, tp),
    )
    gath[mine] = tokens_ref[...]

    gain_col = jnp.broadcast_to(gain1_ref[...], (128, full)).T[:, :1]
    bias_col = jnp.broadcast_to(bias1_ref[...], (128, full)).T[:, :1]
    for copy in token_copies:
        copy.wait_recv()
    wide = gath[...].astype(jnp.float32)
    mean = jnp.sum(wide, axis=0, keepdims=True) / full
    centered = wide - mean
    variance = jnp.sum(centered * centered, axis=0, keepdims=True) / full
    normed[...] = (centered * lax.rsqrt(variance + epsilon) * gain_col + bias_col).astype(
        jnp.bfloat16
    )
    for kind in range(3):
        heads[kind] = (
            dot(qkv_ref[kind], normed[...], (1, 0))
            .astype(jnp.bfloat16)
            .astype(jnp.float32)
            .reshape(4, HEAD_DIM, tok_count)
        )
    to_beside[0].wait_recv()
    relay_above.start()
    to_above[0].wait_recv()
    relay_beside.start()

    part_copies = [
        remote(leaving.at[step - 1], landing.at[step - 1], 8 + step, (req, (tp + step) % 4))
        for step in range(1, 4)
    ]

    def block(step):
        start = pl.multiple_of((tp + step) % 4 * rows, rows)
        window = pl.ds(start, rows)
        allowed = seg_col_ref[...] == seg_row_ref[:, window]
        pieces = []
        for head in range(4):
            query = heads[0, head, :, window].astype(jnp.bfloat16)
            key = heads[1, head].astype(jnp.bfloat16)
            value = heads[2, head].astype(jnp.bfloat16)
            scores = dot(key, query, (0, 0)) * HEAD_DIM ** (-0.5)
            scores = jnp.where(allowed, scores, -1e30)
            exponent = jnp.exp(scores - jnp.max(scores, axis=0, keepdims=True))
            weights = exponent * (1.0 / jnp.sum(exponent, axis=0, keepdims=True))
            pieces.append(dot(value, weights.astype(jnp.bfloat16), (1, 0)))
        context = jnp.concatenate(pieces, axis=0).astype(jnp.bfloat16)
        return dot(context, out_weight_ref[...], (0, 0))

    for step in range(1, 4):
        leaving[step - 1] = block(step).astype(jnp.bfloat16)
        part_copies[step - 1].start()
    own_window = pl.ds(pl.multiple_of(tp * rows, rows), rows)
    own_sum[...] = block(0) + gath[:, own_window].astype(jnp.float32).T
    for copy in part_copies:
        copy.wait_recv()
    hidden = own_sum[...]
    for step in range(3):
        hidden += landing[step].astype(jnp.float32)
    mean = jnp.sum(hidden, axis=1, keepdims=True) / full
    centered = hidden - mean
    variance = jnp.sum(centered * centered, axis=1, keepdims=True) / full
    patches = (
        centered * lax.rsqrt(variance + epsilon) * gain2_ref[...] + bias2_ref[...]
    ).astype(jnp.bfloat16)

    def plane_of(index):
        chosen = 4 * lax.broadcasted_iota(jnp.int32, (part, rows), 0) + index
        picks = jnp.where(lax.broadcasted_iota(jnp.int32, (part, rows), 1) == chosen, 1.0, 0.0)
        return dot(picks.astype(jnp.bfloat16), patches, (1, 0)).astype(jnp.bfloat16)

    own_place = pl.ds(pl.multiple_of(tp * part, part), part)
    far_place = pl.ds(pl.multiple_of(groups + tp * part, part), part)
    for plane in range(2):
        going[plane] = plane_of(2 * (1 - upper) + plane)
    pair_copy = remote(going, merged.at[:, far_place], 12, (across, tp))
    pair_copy.start()
    for plane in range(2):
        merged[plane, own_place] = plane_of(2 * upper + plane)
    near_copies = [
        remote(merged.at[:, own_place], merged.at[:, own_place], 12 + step, (req, (tp + step) % 4))
        for step in range(1, 4)
    ]
    for copy in near_copies:
        copy.start()
    pair_copy.wait_recv()
    far_copies = [
        remote(merged.at[:, far_place], merged.at[:, far_place], 15 + step, (req, (tp + step) % 4))
        for step in range(1, 4)
    ]
    for copy in far_copies:
        copy.start()
    slot_of = own_row_ref[...]
    same = own_col_ref[...] == slot_of
    before = lax.broadcasted_iota(jnp.int32, same.shape, 0) < lax.broadcasted_iota(
        jnp.int32, same.shape, 1
    )
    rank = jnp.sum(jnp.where(same & before, 1.0, 0.0), axis=0, keepdims=True).astype(jnp.int32)
    slot_of = slot_of * capacity + rank
    placing = jnp.where(
        lax.broadcasted_iota(jnp.int32, (8 * capacity, groups), 0) == slot_of, 1.0, 0.0
    ).astype(jnp.bfloat16)
    for copy in near_copies:
        copy.wait_recv()
    own_weight.wait()
    for copy in (to_beside[1], to_above[1], relay_above, relay_beside):
        copy.wait_recv()
    for copy in far_copies:
        copy.wait_recv()
    far_rows, near_rows = pl.ds(groups, groups), pl.ds(0, groups)

    def project(window):
        return dot(merged[0, window], held[:full], (1, 0)) + dot(
            merged[1, window], held[full:], (1, 0)
        )

    half_out[...] = project(far_rows).astype(jnp.bfloat16)
    half_copy = remote(half_out, half_in, 19, (across, tp))
    half_copy.start()
    projected = project(near_rows)
    half_copy.wait_recv()
    projected = (projected + half_in[...].astype(jnp.float32)).astype(jnp.bfloat16)
    outgoing[...] = dot(placing, projected, (1, 0)).astype(jnp.bfloat16)
    landing_rows = pl.ds(pl.multiple_of(req * capacity, capacity), capacity)
    out_copies = []
    for step in range(1, 8):
        owner = (req + step) % 8
        source = outgoing.at[pl.ds(pl.multiple_of(owner * capacity, capacity), capacity)]
        out_copies.append(remote(source, result_ref.at[landing_rows], 19 + step, (owner, tp)))
    for copy in out_copies:
        copy.start()
    result_ref[landing_rows] = outgoing[landing_rows]
    for copy in out_copies:
        copy.wait_recv()
    for copy in (
        token_copies
        + to_beside
        + to_above
        + [relay_above, relay_beside, pair_copy, half_copy]
        + part_copies
        + near_copies
        + far_copies
        + out_copies
    ):
        copy.wait_send()


def in_one_kernel(
    tokens,
    ln1_gain,
    ln1_bias,
    qkv_weight,
    out_weight,
    ln2_gain,
    ln2_bias,
    merger_weight,
    group_segments,
    owners,
):
    tok_count, feats = tokens.shape
    full = 4 * feats
    rows = tok_count // 4
    out_cols = merger_weight.shape[1]
    slots = 8 * max(2, 2 * rows // 8)
    segment_ids = jnp.repeat(group_segments[0], 4)
    bf16, f32 = jnp.bfloat16, jnp.float32
    vmem = pl.BlockSpec(memory_space=pltpu.VMEM)
    return pl.pallas_call(
        kernel,
        out_shape=jax.ShapeDtypeStruct((slots, out_cols), bf16),
        in_specs=[vmem] * 12,
        out_specs=vmem,
        scratch_shapes=[
            pltpu.VMEM((full, tok_count), bf16),
            pltpu.VMEM((full, tok_count), bf16),
            pltpu.VMEM((3, 4, HEAD_DIM, tok_count), f32),
            pltpu.VMEM((3, rows, full), bf16),
            pltpu.VMEM((3, rows, full), bf16),
            pltpu.VMEM((rows, full), f32),
            pltpu.VMEM((2, 2 * rows, full), bf16),
            pltpu.VMEM((2, rows // 4, full), bf16),
            pltpu.VMEM((2 * full, out_cols), bf16),
            pltpu.VMEM((rows, out_cols), bf16),
            pltpu.VMEM((rows, out_cols), bf16),
            pltpu.VMEM((slots, out_cols), bf16),
            pltpu.SemaphoreType.DMA,
            pltpu.SemaphoreType.DMA((27,)),
            pltpu.SemaphoreType.DMA((27,)),
        ],
        compiler_params=pltpu.CompilerParams(
            collective_id=0, has_side_effects=True, vmem_limit_bytes=58 << 20
        ),
    )(
        tokens.T,
        ln1_gain[None],
        ln1_bias[None],
        qkv_weight.transpose(0, 2, 1),
        out_weight,
        ln2_gain[None],
        ln2_bias[None],
        merger_weight,
        segment_ids[:, None],
        segment_ids[None],
        owners,
        owners.reshape(1, -1),
    )


def solution(mesh):
    in_specs = (
        P("req", "tp"),
        P(),
        P(),
        P(None, None, "tp"),
        P("tp", None),
        P(),
        P(),
        P("req", "tp"),
        P("req", None),
        P("req", None),
    )
    out_specs = P("req", "tp")
    sizes = mesh.shape
    body = in_one_kernel if sizes["req"] == 8 and sizes["tp"] == 4 else local
    return jax.shard_map(body, mesh=mesh, in_specs=in_specs, out_specs=out_specs, check_vma=False)
```

```python
import jax
import jax.numpy as jnp
from jax import lax
from jax.experimental import pallas as pl
from jax.experimental.pallas import tpu as pltpu
from jax.sharding import PartitionSpec as P

HEAD_DIM = 88


epsilon = 1e-06


def layer_norm(values, gain, bias):
    mean = jnp.mean(values, axis=1, keepdims=True)
    centered = values - mean
    variance = jnp.mean(centered * centered, axis=1, keepdims=True)
    return (centered * lax.rsqrt(variance + epsilon) * gain + bias).astype(jnp.bfloat16)


def local(
    tokens,
    ln1_gain,
    ln1_bias,
    qkv_weight,
    out_weight,
    ln2_gain,
    ln2_bias,
    merger_weight,
    group_segments,
    owners,
):
    tp_count = lax.axis_size("tp")
    req_count = lax.axis_size("req")
    tp_index = lax.axis_index("tp")
    req_index = lax.axis_index("req")
    half = req_count // 2
    upper = req_index // half
    tok_count = tokens.shape[0]
    width = tokens.shape[1] * tp_count
    row_count = tok_count // tp_count
    group_count = tok_count // 4
    own_groups = group_count // tp_count
    out_cols = merger_weight.shape[1]
    gathered = lax.all_gather(tokens, "tp", axis=1, tiled=True)
    gathered, merger_part = lax.optimization_barrier((gathered, merger_weight))
    halves = [list(range(half)), list(range(half, req_count))]
    kept_weight = lax.all_gather(
        merger_part, "req", axis=0, tiled=True, axis_index_groups=halves
    )
    normed = layer_norm(gathered.astype(jnp.float32), ln1_gain, ln1_bias)
    combined = jnp.einsum("td,cdh->cth", normed, qkv_weight, preferred_element_type=jnp.float32)
    combined = combined.astype(jnp.bfloat16).reshape(3, tok_count, -1, HEAD_DIM)
    queries, key_heads, value_heads = (combined[0], combined[1], combined[2])
    segment_ids = jnp.repeat(group_segments[0], 4)
    same_picture = segment_ids[:, None] == segment_ids[None, :]
    scores = jnp.einsum(
        "qhd,khd->hqk", queries, key_heads, preferred_element_type=jnp.float32
    ) * HEAD_DIM ** (-0.5)
    scores = jnp.where(same_picture[None], scores, -1e30)
    row_max = jnp.max(scores, axis=2, keepdims=True)
    exponent = jnp.exp(scores - row_max)
    weights = (exponent / jnp.sum(exponent, axis=2, keepdims=True)).astype(jnp.bfloat16)
    context = jnp.einsum("hqk,khd->qhd", weights, value_heads, preferred_element_type=jnp.float32)
    context = context.astype(jnp.bfloat16).reshape(tok_count, -1)
    partial_value = jnp.dot(context, out_weight, preferred_element_type=jnp.float32)
    pieces = partial_value.astype(jnp.bfloat16).reshape(tp_count, row_count, width)

    def rows_of(array, index):
        return lax.dynamic_index_in_dim(array, index, 0, keepdims=False)

    hidden = rows_of(gathered.reshape(tp_count, row_count, width), tp_index).astype(jnp.float32)
    hidden += rows_of(partial_value.reshape(tp_count, row_count, width), tp_index)
    for step in range(1, tp_count):
        leaving = rows_of(pieces, (tp_index + step) % tp_count)
        hidden += lax.ppermute(
            leaving, "tp", [(i, (i + step) % tp_count) for i in range(tp_count)]
        ).astype(jnp.float32)
    patches = layer_norm(hidden, ln2_gain, ln2_bias)
    merged = patches.reshape(own_groups, 2, 2 * width)
    swap = [(i, (i + half) % req_count) for i in range(req_count)]
    staying = lax.dynamic_index_in_dim(merged, upper, 1, keepdims=False)
    going = lax.dynamic_index_in_dim(merged, 1 - upper, 1, keepdims=False)
    coming = lax.ppermute(going, "req", swap)
    both = jnp.stack([staying, coming])
    full = lax.all_gather(both, "tp", axis=1, tiled=True)
    projected = jnp.dot(
        full.reshape(2 * group_count, 2 * width),
        kept_weight,
        preferred_element_type=jnp.float32,
    )
    arriving = lax.ppermute(projected[group_count:].astype(jnp.bfloat16), "req", swap)
    projected = projected[:group_count] + arriving.astype(jnp.float32)
    projected = projected.astype(jnp.bfloat16)
    capacity = max(2, 2 * group_count // req_count)
    slot_count = req_count * capacity
    target = owners[:, 0]
    same_owner = target[:, None] == target[None, :]
    place = jnp.arange(group_count, dtype=jnp.int32)
    earlier = same_owner & (place[None, :] < place[:, None])
    slot_rank = jnp.sum(earlier.astype(jnp.int32), axis=1)
    slot_index = target * capacity + slot_rank
    placing = (slot_index[None, :] == jnp.arange(slot_count, dtype=jnp.int32)[:, None]).astype(
        jnp.bfloat16
    )
    outgoing = jnp.dot(placing, projected, preferred_element_type=jnp.float32).astype(jnp.bfloat16)
    outgoing = outgoing.reshape(req_count, capacity, out_cols)
    arrived = lax.all_to_all(outgoing, "req", split_axis=0, concat_axis=0, tiled=True)
    return arrived.reshape(slot_count, out_cols)


def dot(left, right, contract):
    return lax.dot_general(
        left, right, ((contract[:1], contract[1:]), ((), ())), preferred_element_type=jnp.float32
    )


def kernel(
    tokens_ref,
    gain1_ref,
    bias1_ref,
    qkv_ref,
    out_weight_ref,
    gain2_ref,
    bias2_ref,
    merger_ref,
    seg_ref,
    own_ref,
    result_ref,
    qkv_held,
    out_held,
    gath,
    normed,
    heads,
    leaving,
    landing,
    own_sum,
    merged,
    going,
    held,
    seg_tok,
    placing,
    projected,
    half_out,
    half_in,
    outgoing,
    local_sem,
    send_sem,
    recv_sem,
):
    tp = lax.axis_index("tp")
    req = lax.axis_index("req")
    feats, tok_count = tokens_ref.shape
    full = gath.shape[0]
    rows = tok_count // 4
    groups = tok_count // 4
    part = rows // 4
    shard = merger_ref.shape[0]
    cut = shard // 2
    place = req % 4
    upper = req // 4
    across = (req + 4) % 8
    beside = req + 1 - 2 * (req % 2)
    above = req - place + (place + 2) % 4
    capacity = result_ref.shape[0] // 8

    def remote(source, target, index, device):
        return pltpu.make_async_remote_copy(
            src_ref=source,
            dst_ref=target,
            send_sem=send_sem.at[index],
            recv_sem=recv_sem.at[index],
            device_id=device,
            device_id_type=pl.DeviceIdType.MESH,
        )

    sibling = tp + 1 - 2 * (tp % 2)
    facing = (tp + 2) % 4
    corner = (sibling + 2) % 4
    qkv_copy = pltpu.make_async_copy(qkv_ref, qkv_held, local_sem.at[1])
    qkv_copy.start()
    out_copy = pltpu.make_async_copy(out_weight_ref, out_held, local_sem.at[2])
    out_copy.start()
    barrier = pltpu.get_barrier_semaphore()
    for peer in (sibling, facing):
        pl.semaphore_signal(
            barrier, inc=1, device_id=(req, peer), device_id_type=pl.DeviceIdType.MESH
        )
    for step in range(1, 8):
        pl.semaphore_signal(
            barrier, inc=1, device_id=((req + step) % 8, tp), device_id_type=pl.DeviceIdType.MESH
        )
    pl.semaphore_wait(barrier, 9)

    mine = pl.ds(pl.multiple_of(tp * feats, 16), feats)
    theirs = pl.ds(pl.multiple_of(facing * feats, 16), feats)
    token_copies = [
        remote(tokens_ref, gath.at[mine], 1, (req, facing)),
        remote(tokens_ref, gath.at[mine], 0, (req, sibling)),
        remote(gath.at[theirs], gath.at[theirs], 2, (req, sibling)),
    ]
    for copy in token_copies[:2]:
        copy.start()

    def weight_rows(owner, lower):
        return pl.ds(pl.multiple_of(owner * shard + lower * cut, 16), cut)

    first, second = merger_ref.at[pl.ds(0, cut)], merger_ref.at[pl.ds(cut, cut)]
    to_beside = [
        remote(first, held.at[weight_rows(place, 0)], 3, (beside, tp)),
        remote(second, held.at[weight_rows(place, 1)], 4, (beside, tp)),
    ]
    to_above = [
        remote(second, held.at[weight_rows(place, 1)], 5, (above, tp)),
        remote(first, held.at[weight_rows(place, 0)], 6, (above, tp)),
    ]
    to_beside[0].start()
    to_above[0].start()
    to_beside[1].start()
    to_above[1].start()
    own_weight = pltpu.make_async_copy(
        merger_ref, held.at[pl.ds(pl.multiple_of(place * shard, 16), shard)], local_sem.at[0]
    )
    own_weight.start()
    beside_place, above_place = beside % 4, above % 4
    relay_above = remote(
        held.at[weight_rows(beside_place, 0)],
        held.at[weight_rows(beside_place, 0)],
        7,
        (above, tp),
    )
    relay_beside = remote(
        held.at[weight_rows(above_place, 1)],
        held.at[weight_rows(above_place, 1)],
        8,
        (beside, tp),
    )
    gath[mine] = tokens_ref[...]

    def column(row, amount):
        return jnp.broadcast_to(row, (128, amount)).T[:, :1]

    gain_col = column(gain1_ref[...].reshape(1, full), full)
    bias_col = column(bias1_ref[...].reshape(1, full), full)
    seg_row = seg_ref[...].astype(jnp.float32)
    tall, long = (tok_count, groups), (groups, tok_count)
    spread = lax.broadcasted_iota(jnp.int32, tall, 1) == lax.shift_right_logical(
        lax.broadcasted_iota(jnp.int32, tall, 0), 2
    )
    seg_col_tok = jnp.sum(jnp.where(spread, seg_row, 0.0), axis=1, keepdims=True)
    spread = lax.broadcasted_iota(jnp.int32, long, 0) == lax.shift_right_logical(
        lax.broadcasted_iota(jnp.int32, long, 1), 2
    )
    seg_tok[...] = jnp.sum(
        jnp.where(spread, column(seg_row, groups), 0.0), axis=0, keepdims=True
    )
    slot_of = own_ref[...]
    same = column(slot_of.astype(jnp.float32), groups) == slot_of.astype(jnp.float32)
    before = lax.broadcasted_iota(jnp.int32, same.shape, 0) < lax.broadcasted_iota(
        jnp.int32, same.shape, 1
    )
    rank = jnp.sum(jnp.where(same & before, 1.0, 0.0), axis=0, keepdims=True).astype(jnp.int32)
    slot_of = slot_of * capacity + rank
    placing[...] = jnp.where(
        lax.broadcasted_iota(jnp.int32, (8 * capacity, groups), 0) == slot_of, 1.0, 0.0
    ).astype(jnp.bfloat16)
    token_copies[0].wait_recv()
    token_copies[2].start()
    token_copies[1].wait_recv()
    token_copies[2].wait_recv()
    wide = gath[...].astype(jnp.float32)
    mean = jnp.sum(wide, axis=0, keepdims=True) / full
    centered = wide - mean
    variance = jnp.sum(centered * centered, axis=0, keepdims=True) / full
    normed[...] = (centered * lax.rsqrt(variance + epsilon) * gain_col + bias_col).astype(
        jnp.bfloat16
    )
    qkv_copy.wait()
    for kind in range(3):
        heads[kind] = (
            dot(qkv_held[kind], normed[...], (1, 0))
            .astype(jnp.bfloat16)
            .astype(jnp.float32)
            .reshape(4, HEAD_DIM, tok_count)
        )
    to_beside[0].wait_recv()
    relay_above.start()
    to_above[0].wait_recv()
    relay_beside.start()

    part_copies = [
        remote(leaving.at[0], landing.at[0], 9, (req, sibling)),
        remote(leaving.at[1], landing.at[1], 10, (req, facing)),
        remote(leaving.at[2], landing.at[2], 11, (req, sibling)),
    ]
    out_copy.wait()

    def block(owner):
        start = pl.multiple_of(owner * rows, rows)
        window = pl.ds(start, rows)
        allowed = seg_col_tok == seg_tok[:, window]
        pieces = []
        for head in range(4):
            query = heads[0, head, :, window].astype(jnp.bfloat16)
            key = heads[1, head].astype(jnp.bfloat16)
            value = heads[2, head].astype(jnp.bfloat16)
            scores = dot(key, query, (0, 0)) * HEAD_DIM ** (-0.5)
            scores = jnp.where(allowed, scores, -1e30)
            exponent = jnp.exp(scores - jnp.max(scores, axis=0, keepdims=True))
            weights = exponent * (1.0 / jnp.sum(exponent, axis=0, keepdims=True))
            pieces.append(dot(value, weights.astype(jnp.bfloat16), (1, 0)))
        context = jnp.concatenate(pieces, axis=0).astype(jnp.bfloat16)
        return dot(context, out_held[...], (0, 0))

    leaving[0] = block(corner).astype(jnp.bfloat16)
    part_copies[0].start()
    crossing = block(facing)
    part_copies[0].wait_recv()
    leaving[1] = (crossing + landing[0].astype(jnp.float32)).astype(jnp.bfloat16)
    part_copies[1].start()
    leaving[2] = block(sibling).astype(jnp.bfloat16)
    part_copies[2].start()
    own_window = pl.ds(pl.multiple_of(tp * rows, rows), rows)
    own_sum[...] = block(tp) + gath[:, own_window].astype(jnp.float32).T
    for copy in part_copies[1:]:
        copy.wait_recv()
    hidden = own_sum[...]
    for step in range(1, 3):
        hidden += landing[step].astype(jnp.float32)
    mean = jnp.sum(hidden, axis=1, keepdims=True) / full
    centered = hidden - mean
    variance = jnp.sum(centered * centered, axis=1, keepdims=True) / full
    patches = (
        centered * lax.rsqrt(variance + epsilon) * gain2_ref[...].reshape(1, full) + bias2_ref[...].reshape(1, full)
    ).astype(jnp.bfloat16)

    def plane_of(index):
        chosen = 4 * lax.broadcasted_iota(jnp.int32, (part, rows), 0) + index
        picks = jnp.where(lax.broadcasted_iota(jnp.int32, (part, rows), 1) == chosen, 1.0, 0.0)
        return dot(picks.astype(jnp.bfloat16), patches, (1, 0)).astype(jnp.bfloat16)

    own_place = pl.ds(pl.multiple_of(tp * part, part), part)
    far_place = pl.ds(pl.multiple_of(groups + tp * part, part), part)
    for plane in range(2):
        going[plane] = plane_of(2 * (1 - upper) + plane)
    pair_copy = remote(going, merged.at[:, far_place], 12, (across, tp))
    pair_copy.start()
    for plane in range(2):
        merged[plane, own_place] = plane_of(2 * upper + plane)
    facing_place = pl.ds(pl.multiple_of(facing * part, part), part)
    facing_far = pl.ds(pl.multiple_of(groups + facing * part, part), part)

    def spreading(own, other, index):
        return [
            remote(merged.at[:, own], merged.at[:, own], index, (req, facing)),
            remote(merged.at[:, own], merged.at[:, own], index + 1, (req, sibling)),
            remote(merged.at[:, other], merged.at[:, other], index + 2, (req, sibling)),
        ]

    near_copies = spreading(own_place, facing_place, 13)
    far_copies = spreading(far_place, facing_far, 16)
    near_copies[0].start()
    near_copies[1].start()
    near_copies[0].wait_recv()
    near_copies[2].start()
    pair_copy.wait_recv()
    far_copies[0].start()
    far_copies[1].start()
    near_copies[1].wait_recv()
    near_copies[2].wait_recv()
    own_weight.wait()
    for copy in (to_beside[1], to_above[1], relay_above, relay_beside):
        copy.wait_recv()
    far_rows, near_rows = pl.ds(groups, groups), pl.ds(0, groups)

    def project(window, cols):
        return dot(merged[0, window], held[:full, cols], (1, 0)) + dot(
            merged[1, window], held[full:, cols], (1, 0)
        )

    out_cols = result_ref.shape[1]
    middle = 512
    column_parts = [pl.ds(0, middle), pl.ds(middle, out_cols - middle)]
    for cols in column_parts:
        projected[:, cols] = project(near_rows, cols)
    far_copies[0].wait_recv()
    far_copies[2].start()
    far_copies[1].wait_recv()
    far_copies[2].wait_recv()
    half_copies = []
    for index, cols in enumerate(column_parts):
        half_out[:, cols] = project(far_rows, cols).astype(jnp.bfloat16)
        copy = remote(half_out.at[:, cols], half_in.at[:, cols], 19 + index, (across, tp))
        copy.start()
        half_copies.append(copy)
    landing_rows = pl.ds(pl.multiple_of(req * capacity, capacity), capacity)
    out_copies = []
    for index, cols in enumerate(column_parts):
        half_copies[index].wait_recv()
        summed = projected[:, cols] + half_in[:, cols].astype(jnp.float32)
        outgoing[:, cols] = dot(placing[...], summed.astype(jnp.bfloat16), (1, 0)).astype(
            jnp.bfloat16
        )
        for step in (4, 6, 2, 5, 3, 7, 1):
            owner = (req + step) % 8
            source = pl.ds(pl.multiple_of(owner * capacity, capacity), capacity)
            copy = remote(
                outgoing.at[source, cols],
                result_ref.at[landing_rows, cols],
                20 + 7 * index + step,
                (owner, tp),
            )
            copy.start()
            out_copies.append(copy)
    result_ref[landing_rows] = outgoing[landing_rows]
    for copy in out_copies:
        copy.wait_recv()
    for copy in (
        token_copies
        + to_beside
        + to_above
        + [relay_above, relay_beside, pair_copy]
        + half_copies
        + part_copies
        + near_copies
        + far_copies
        + out_copies
    ):
        copy.wait_send()


def in_one_kernel(
    tokens,
    ln1_gain,
    ln1_bias,
    qkv_weight,
    out_weight,
    ln2_gain,
    ln2_bias,
    merger_weight,
    group_segments,
    owners,
):
    tok_count, feats = tokens.shape
    full = 4 * feats
    rows = tok_count // 4
    out_cols = merger_weight.shape[1]
    slots = 8 * max(2, 2 * rows // 8)
    bf16, f32 = jnp.bfloat16, jnp.float32
    anywhere = pl.BlockSpec(memory_space=pl.ANY)
    vmem = pl.BlockSpec(memory_space=pltpu.VMEM)
    return pl.pallas_call(
        kernel,
        out_shape=jax.ShapeDtypeStruct((slots, out_cols), bf16),
        in_specs=[vmem] * 3 + [anywhere] * 2 + [vmem] * 2 + [anywhere] + [vmem] * 2,
        out_specs=vmem,
        scratch_shapes=[
            pltpu.VMEM((3, feats, full), bf16),
            pltpu.VMEM((feats, full), bf16),
            pltpu.VMEM((full, tok_count), bf16),
            pltpu.VMEM((full, tok_count), bf16),
            pltpu.VMEM((3, 4, HEAD_DIM, tok_count), f32),
            pltpu.VMEM((3, rows, full), bf16),
            pltpu.VMEM((3, rows, full), bf16),
            pltpu.VMEM((rows, full), f32),
            pltpu.VMEM((2, 2 * rows, full), bf16),
            pltpu.VMEM((2, rows // 4, full), bf16),
            pltpu.VMEM((2 * full, out_cols), bf16),
            pltpu.VMEM((1, tok_count), f32),
            pltpu.VMEM((slots, rows), bf16),
            pltpu.VMEM((rows, out_cols), f32),
            pltpu.VMEM((rows, out_cols), bf16),
            pltpu.VMEM((rows, out_cols), bf16),
            pltpu.VMEM((slots, out_cols), bf16),
            pltpu.SemaphoreType.DMA((3,)),
            pltpu.SemaphoreType.DMA((35,)),
            pltpu.SemaphoreType.DMA((35,)),
        ],
        compiler_params=pltpu.CompilerParams(
            collective_id=0, has_side_effects=True, vmem_limit_bytes=58 << 20
        ),
    )(
        tokens.T,
        ln1_gain,
        ln1_bias,
        qkv_weight.transpose(0, 2, 1),
        out_weight,
        ln2_gain,
        ln2_bias,
        merger_weight,
        group_segments,
        owners.reshape(1, -1),
    )


def solution(mesh):
    in_specs = (
        P("req", "tp"),
        P(),
        P(),
        P(None, None, "tp"),
        P("tp", None),
        P(),
        P(),
        P("req", "tp"),
        P("req", None),
        P("req", None),
    )
    out_specs = P("req", "tp")
    sizes = mesh.shape
    body = in_one_kernel if sizes["req"] == 8 and sizes["tp"] == 4 else local
    return jax.shard_map(body, mesh=mesh, in_specs=in_specs, out_specs=out_specs, check_vma=False)
```

```python
import jax
import jax.numpy as jnp
from jax import lax
from jax.experimental import pallas as pl
from jax.experimental.pallas import tpu as pltpu
from jax.sharding import PartitionSpec as P

HEAD_DIM = 88


epsilon = 1e-06


def layer_norm(values, gain, bias):
    mean = jnp.mean(values, axis=1, keepdims=True)
    centered = values - mean
    variance = jnp.mean(centered * centered, axis=1, keepdims=True)
    return (centered * lax.rsqrt(variance + epsilon) * gain + bias).astype(jnp.bfloat16)


def local(
    tokens,
    ln1_gain,
    ln1_bias,
    qkv_weight,
    out_weight,
    ln2_gain,
    ln2_bias,
    merger_weight,
    group_segments,
    owners,
):
    tp_count = lax.axis_size("tp")
    req_count = lax.axis_size("req")
    tp_index = lax.axis_index("tp")
    req_index = lax.axis_index("req")
    half = req_count // 2
    upper = req_index // half
    tok_count = tokens.shape[0]
    width = tokens.shape[1] * tp_count
    row_count = tok_count // tp_count
    group_count = tok_count // 4
    own_groups = group_count // tp_count
    out_cols = merger_weight.shape[1]
    gathered = lax.all_gather(tokens, "tp", axis=1, tiled=True)
    gathered, merger_part = lax.optimization_barrier((gathered, merger_weight))
    halves = [list(range(half)), list(range(half, req_count))]
    kept_weight = lax.all_gather(
        merger_part, "req", axis=0, tiled=True, axis_index_groups=halves
    )
    normed = layer_norm(gathered.astype(jnp.float32), ln1_gain, ln1_bias)
    combined = jnp.einsum("td,cdh->cth", normed, qkv_weight, preferred_element_type=jnp.float32)
    combined = combined.astype(jnp.bfloat16).reshape(3, tok_count, -1, HEAD_DIM)
    queries, key_heads, value_heads = (combined[0], combined[1], combined[2])
    segment_ids = jnp.repeat(group_segments[0], 4)
    same_picture = segment_ids[:, None] == segment_ids[None, :]
    scores = jnp.einsum(
        "qhd,khd->hqk", queries, key_heads, preferred_element_type=jnp.float32
    ) * HEAD_DIM ** (-0.5)
    scores = jnp.where(same_picture[None], scores, -1e30)
    row_max = jnp.max(scores, axis=2, keepdims=True)
    exponent = jnp.exp(scores - row_max)
    weights = (exponent / jnp.sum(exponent, axis=2, keepdims=True)).astype(jnp.bfloat16)
    context = jnp.einsum("hqk,khd->qhd", weights, value_heads, preferred_element_type=jnp.float32)
    context = context.astype(jnp.bfloat16).reshape(tok_count, -1)
    partial_value = jnp.dot(context, out_weight, preferred_element_type=jnp.float32)
    pieces = partial_value.astype(jnp.bfloat16).reshape(tp_count, row_count, width)

    def rows_of(array, index):
        return lax.dynamic_index_in_dim(array, index, 0, keepdims=False)

    hidden = rows_of(gathered.reshape(tp_count, row_count, width), tp_index).astype(jnp.float32)
    hidden += rows_of(partial_value.reshape(tp_count, row_count, width), tp_index)
    for step in range(1, tp_count):
        leaving = rows_of(pieces, (tp_index + step) % tp_count)
        hidden += lax.ppermute(
            leaving, "tp", [(i, (i + step) % tp_count) for i in range(tp_count)]
        ).astype(jnp.float32)
    patches = layer_norm(hidden, ln2_gain, ln2_bias)
    merged = patches.reshape(own_groups, 2, 2 * width)
    swap = [(i, (i + half) % req_count) for i in range(req_count)]
    staying = lax.dynamic_index_in_dim(merged, upper, 1, keepdims=False)
    going = lax.dynamic_index_in_dim(merged, 1 - upper, 1, keepdims=False)
    coming = lax.ppermute(going, "req", swap)
    both = jnp.stack([staying, coming])
    full = lax.all_gather(both, "tp", axis=1, tiled=True)
    projected = jnp.dot(
        full.reshape(2 * group_count, 2 * width),
        kept_weight,
        preferred_element_type=jnp.float32,
    )
    arriving = lax.ppermute(projected[group_count:].astype(jnp.bfloat16), "req", swap)
    projected = projected[:group_count] + arriving.astype(jnp.float32)
    projected = projected.astype(jnp.bfloat16)
    capacity = max(2, 2 * group_count // req_count)
    slot_count = req_count * capacity
    target = owners[:, 0]
    same_owner = target[:, None] == target[None, :]
    place = jnp.arange(group_count, dtype=jnp.int32)
    earlier = same_owner & (place[None, :] < place[:, None])
    slot_rank = jnp.sum(earlier.astype(jnp.int32), axis=1)
    slot_index = target * capacity + slot_rank
    placing = (slot_index[None, :] == jnp.arange(slot_count, dtype=jnp.int32)[:, None]).astype(
        jnp.bfloat16
    )
    outgoing = jnp.dot(placing, projected, preferred_element_type=jnp.float32).astype(jnp.bfloat16)
    outgoing = outgoing.reshape(req_count, capacity, out_cols)
    arrived = lax.all_to_all(outgoing, "req", split_axis=0, concat_axis=0, tiled=True)
    return arrived.reshape(slot_count, out_cols)


def dot(left, right, contract):
    return lax.dot_general(
        left, right, ((contract[:1], contract[1:]), ((), ())), preferred_element_type=jnp.float32
    )


def kernel(
    tokens_ref,
    gain1_ref,
    bias1_ref,
    qkv_ref,
    out_weight_ref,
    gain2_ref,
    bias2_ref,
    merger_ref,
    seg_ref,
    own_ref,
    result_ref,
    qkv_held,
    out_held,
    gath,
    normed,
    heads,
    leaving,
    landing,
    own_sum,
    merged,
    going,
    held,
    seg_tok,
    placing,
    projected,
    half_out,
    half_in,
    outgoing,
    local_sem,
    send_sem,
    recv_sem,
):
    tp = lax.axis_index("tp")
    req = lax.axis_index("req")
    feats, tok_count = tokens_ref.shape
    full = gath.shape[0]
    rows = tok_count // 4
    groups = tok_count // 4
    part = rows // 4
    shard = merger_ref.shape[0]
    cut = shard // 2
    place = req % 4
    upper = req // 4
    across = (req + 4) % 8
    beside = req + 1 - 2 * (req % 2)
    above = req - place + (place + 2) % 4
    capacity = result_ref.shape[0] // 8

    def remote(source, target, index, device):
        return pltpu.make_async_remote_copy(
            src_ref=source,
            dst_ref=target,
            send_sem=send_sem.at[index],
            recv_sem=recv_sem.at[index],
            device_id=device,
            device_id_type=pl.DeviceIdType.MESH,
        )

    sibling = tp + 1 - 2 * (tp % 2)
    facing = (tp + 2) % 4
    corner = (sibling + 2) % 4
    qkv_copy = pltpu.make_async_copy(qkv_ref, qkv_held, local_sem.at[1])
    qkv_copy.start()
    out_copy = pltpu.make_async_copy(out_weight_ref, out_held, local_sem.at[2])
    out_copy.start()
    barrier = pltpu.get_barrier_semaphore()
    for peer in (sibling, facing):
        pl.semaphore_signal(
            barrier, inc=1, device_id=(req, peer), device_id_type=pl.DeviceIdType.MESH
        )
    for step in range(1, 8):
        pl.semaphore_signal(
            barrier, inc=1, device_id=((req + step) % 8, tp), device_id_type=pl.DeviceIdType.MESH
        )
    pl.semaphore_wait(barrier, 9)

    mine = pl.ds(pl.multiple_of(tp * feats, 16), feats)
    theirs = pl.ds(pl.multiple_of(facing * feats, 16), feats)
    token_copies = [
        remote(tokens_ref, gath.at[mine], 1, (req, facing)),
        remote(tokens_ref, gath.at[mine], 0, (req, sibling)),
        remote(gath.at[theirs], gath.at[theirs], 2, (req, sibling)),
    ]
    for copy in token_copies[:2]:
        copy.start()

    def weight_rows(owner, lower):
        return pl.ds(pl.multiple_of(owner * shard + lower * cut, 16), cut)

    first, second = merger_ref.at[pl.ds(0, cut)], merger_ref.at[pl.ds(cut, cut)]
    to_beside = [
        remote(first, held.at[weight_rows(place, 0)], 3, (beside, tp)),
        remote(second, held.at[weight_rows(place, 1)], 4, (beside, tp)),
    ]
    to_above = [
        remote(second, held.at[weight_rows(place, 1)], 5, (above, tp)),
        remote(first, held.at[weight_rows(place, 0)], 6, (above, tp)),
    ]
    to_beside[0].start()
    to_above[0].start()
    own_weight = pltpu.make_async_copy(
        merger_ref, held.at[pl.ds(pl.multiple_of(place * shard, 16), shard)], local_sem.at[0]
    )
    own_weight.start()
    beside_place, above_place = beside % 4, above % 4
    relay_above = remote(
        held.at[weight_rows(beside_place, 0)],
        held.at[weight_rows(beside_place, 0)],
        7,
        (above, tp),
    )
    relay_beside = remote(
        held.at[weight_rows(above_place, 1)],
        held.at[weight_rows(above_place, 1)],
        8,
        (beside, tp),
    )
    gath[mine] = tokens_ref[...]

    def column(row, amount):
        return jnp.broadcast_to(row, (128, amount)).T[:, :1]

    gain_col = column(gain1_ref[...].reshape(1, full), full)
    bias_col = column(bias1_ref[...].reshape(1, full), full)
    seg_row = seg_ref[...].astype(jnp.float32)
    tall, long = (tok_count, groups), (groups, tok_count)
    spread = lax.broadcasted_iota(jnp.int32, tall, 1) == lax.shift_right_logical(
        lax.broadcasted_iota(jnp.int32, tall, 0), 2
    )
    seg_col_tok = jnp.sum(jnp.where(spread, seg_row, 0.0), axis=1, keepdims=True)
    spread = lax.broadcasted_iota(jnp.int32, long, 0) == lax.shift_right_logical(
        lax.broadcasted_iota(jnp.int32, long, 1), 2
    )
    seg_tok[...] = jnp.sum(
        jnp.where(spread, column(seg_row, groups), 0.0), axis=0, keepdims=True
    )
    slot_of = own_ref[...]
    same = column(slot_of.astype(jnp.float32), groups) == slot_of.astype(jnp.float32)
    before = lax.broadcasted_iota(jnp.int32, same.shape, 0) < lax.broadcasted_iota(
        jnp.int32, same.shape, 1
    )
    rank = jnp.sum(jnp.where(same & before, 1.0, 0.0), axis=0, keepdims=True).astype(jnp.int32)
    slot_of = slot_of * capacity + rank
    placing[...] = jnp.where(
        lax.broadcasted_iota(jnp.int32, (8 * capacity, groups), 0) == slot_of, 1.0, 0.0
    ).astype(jnp.bfloat16)
    token_copies[0].wait_recv()
    token_copies[2].start()
    token_copies[1].wait_recv()
    token_copies[2].wait_recv()
    wide = gath[...].astype(jnp.float32)
    mean = jnp.sum(wide, axis=0, keepdims=True) / full
    centered = wide - mean
    variance = jnp.sum(centered * centered, axis=0, keepdims=True) / full
    normed[...] = (centered * lax.rsqrt(variance + epsilon) * gain_col + bias_col).astype(
        jnp.bfloat16
    )
    to_beside[1].start()
    to_above[1].start()
    qkv_copy.wait()
    for kind in range(3):
        heads[kind] = (
            dot(qkv_held[kind], normed[...], (1, 0))
            .astype(jnp.bfloat16)
            .astype(jnp.float32)
            .reshape(4, HEAD_DIM, tok_count)
        )

    part_copies = [
        remote(leaving.at[0], landing.at[0], 9, (req, sibling)),
        remote(leaving.at[1], landing.at[1], 10, (req, facing)),
        remote(leaving.at[2], landing.at[2], 11, (req, sibling)),
    ]
    out_copy.wait()

    def block(owner):
        start = pl.multiple_of(owner * rows, rows)
        window = pl.ds(start, rows)
        allowed = seg_col_tok == seg_tok[:, window]
        pieces = []
        for head in range(4):
            query = heads[0, head, :, window].astype(jnp.bfloat16)
            key = heads[1, head].astype(jnp.bfloat16)
            value = heads[2, head].astype(jnp.bfloat16)
            scores = dot(key, query, (0, 0)) * HEAD_DIM ** (-0.5)
            scores = jnp.where(allowed, scores, -1e30)
            exponent = jnp.exp(scores - jnp.max(scores, axis=0, keepdims=True))
            weights = exponent * (1.0 / jnp.sum(exponent, axis=0, keepdims=True))
            pieces.append(dot(value, weights.astype(jnp.bfloat16), (1, 0)))
        context = jnp.concatenate(pieces, axis=0).astype(jnp.bfloat16)
        return dot(context, out_held[...], (0, 0))

    leaving[0] = block(corner).astype(jnp.bfloat16)
    part_copies[0].start()
    to_beside[0].wait_recv()
    relay_above.start()
    to_above[0].wait_recv()
    relay_beside.start()
    crossing = block(facing)
    part_copies[0].wait_recv()
    leaving[1] = (crossing + landing[0].astype(jnp.float32)).astype(jnp.bfloat16)
    part_copies[1].start()
    leaving[2] = block(sibling).astype(jnp.bfloat16)
    part_copies[2].start()
    own_window = pl.ds(pl.multiple_of(tp * rows, rows), rows)
    own_sum[...] = block(tp) + gath[:, own_window].astype(jnp.float32).T
    for copy in part_copies[1:]:
        copy.wait_recv()
    hidden = own_sum[...]
    for step in range(1, 3):
        hidden += landing[step].astype(jnp.float32)
    mean = jnp.sum(hidden, axis=1, keepdims=True) / full
    centered = hidden - mean
    variance = jnp.sum(centered * centered, axis=1, keepdims=True) / full
    patches = (
        centered * lax.rsqrt(variance + epsilon) * gain2_ref[...].reshape(1, full) + bias2_ref[...].reshape(1, full)
    ).astype(jnp.bfloat16)

    def plane_of(index):
        chosen = 4 * lax.broadcasted_iota(jnp.int32, (part, rows), 0) + index
        picks = jnp.where(lax.broadcasted_iota(jnp.int32, (part, rows), 1) == chosen, 1.0, 0.0)
        return dot(picks.astype(jnp.bfloat16), patches, (1, 0)).astype(jnp.bfloat16)

    own_place = pl.ds(pl.multiple_of(tp * part, part), part)
    far_place = pl.ds(pl.multiple_of(groups + tp * part, part), part)
    for plane in range(2):
        going[plane] = plane_of(2 * (1 - upper) + plane)
    pair_copy = remote(going, merged.at[:, far_place], 12, (across, tp))
    pair_copy.start()
    for plane in range(2):
        merged[plane, own_place] = plane_of(2 * upper + plane)
    facing_place = pl.ds(pl.multiple_of(facing * part, part), part)
    facing_far = pl.ds(pl.multiple_of(groups + facing * part, part), part)

    def spreading(own, other, index):
        return [
            remote(merged.at[:, own], merged.at[:, own], index, (req, facing)),
            remote(merged.at[:, own], merged.at[:, own], index + 1, (req, sibling)),
            remote(merged.at[:, other], merged.at[:, other], index + 2, (req, sibling)),
        ]

    near_copies = spreading(own_place, facing_place, 13)
    far_copies = spreading(far_place, facing_far, 16)
    near_copies[0].start()
    near_copies[1].start()
    near_copies[0].wait_recv()
    near_copies[2].start()
    pair_copy.wait_recv()
    far_copies[0].start()
    far_copies[1].start()
    near_copies[1].wait_recv()
    near_copies[2].wait_recv()
    own_weight.wait()
    for copy in (to_beside[1], to_above[1], relay_above, relay_beside):
        copy.wait_recv()
    far_rows, near_rows = pl.ds(groups, groups), pl.ds(0, groups)

    def project(window, cols):
        return dot(merged[0, window], held[:full, cols], (1, 0)) + dot(
            merged[1, window], held[full:, cols], (1, 0)
        )

    out_cols = result_ref.shape[1]
    middle = 512
    column_parts = [pl.ds(0, middle), pl.ds(middle, out_cols - middle)]
    for cols in column_parts:
        projected[:, cols] = project(near_rows, cols)
    far_copies[0].wait_recv()
    far_copies[2].start()
    far_copies[1].wait_recv()
    far_copies[2].wait_recv()
    half_copies = []
    for index, cols in enumerate(column_parts):
        half_out[:, cols] = project(far_rows, cols).astype(jnp.bfloat16)
        copy = remote(half_out.at[:, cols], half_in.at[:, cols], 19 + index, (across, tp))
        copy.start()
        half_copies.append(copy)
    landing_rows = pl.ds(pl.multiple_of(req * capacity, capacity), capacity)
    out_copies = []
    for index, cols in enumerate(column_parts):
        half_copies[index].wait_recv()
        summed = projected[:, cols] + half_in[:, cols].astype(jnp.float32)
        outgoing[:, cols] = dot(placing[...], summed.astype(jnp.bfloat16), (1, 0)).astype(
            jnp.bfloat16
        )
        for step in (4, 6, 2, 5, 3, 7, 1):
            owner = (req + step) % 8
            source = pl.ds(pl.multiple_of(owner * capacity, capacity), capacity)
            copy = remote(
                outgoing.at[source, cols],
                result_ref.at[landing_rows, cols],
                20 + 7 * index + step,
                (owner, tp),
            )
            copy.start()
            out_copies.append(copy)
    result_ref[landing_rows] = outgoing[landing_rows]
    for copy in out_copies:
        copy.wait_recv()
    for copy in (
        token_copies
        + to_beside
        + to_above
        + [relay_above, relay_beside, pair_copy]
        + half_copies
        + part_copies
        + near_copies
        + far_copies
        + out_copies
    ):
        copy.wait_send()


def in_one_kernel(
    tokens,
    ln1_gain,
    ln1_bias,
    qkv_weight,
    out_weight,
    ln2_gain,
    ln2_bias,
    merger_weight,
    group_segments,
    owners,
):
    tok_count, feats = tokens.shape
    full = 4 * feats
    rows = tok_count // 4
    out_cols = merger_weight.shape[1]
    slots = 8 * max(2, 2 * rows // 8)
    bf16, f32 = jnp.bfloat16, jnp.float32
    anywhere = pl.BlockSpec(memory_space=pl.ANY)
    vmem = pl.BlockSpec(memory_space=pltpu.VMEM)
    return pl.pallas_call(
        kernel,
        out_shape=jax.ShapeDtypeStruct((slots, out_cols), bf16),
        in_specs=[vmem] * 3 + [anywhere] * 2 + [vmem] * 2 + [anywhere] + [vmem] * 2,
        out_specs=vmem,
        scratch_shapes=[
            pltpu.VMEM((3, feats, full), bf16),
            pltpu.VMEM((feats, full), bf16),
            pltpu.VMEM((full, tok_count), bf16),
            pltpu.VMEM((full, tok_count), bf16),
            pltpu.VMEM((3, 4, HEAD_DIM, tok_count), f32),
            pltpu.VMEM((3, rows, full), bf16),
            pltpu.VMEM((3, rows, full), bf16),
            pltpu.VMEM((rows, full), f32),
            pltpu.VMEM((2, 2 * rows, full), bf16),
            pltpu.VMEM((2, rows // 4, full), bf16),
            pltpu.VMEM((2 * full, out_cols), bf16),
            pltpu.VMEM((1, tok_count), f32),
            pltpu.VMEM((slots, rows), bf16),
            pltpu.VMEM((rows, out_cols), f32),
            pltpu.VMEM((rows, out_cols), bf16),
            pltpu.VMEM((rows, out_cols), bf16),
            pltpu.VMEM((slots, out_cols), bf16),
            pltpu.SemaphoreType.DMA((3,)),
            pltpu.SemaphoreType.DMA((35,)),
            pltpu.SemaphoreType.DMA((35,)),
        ],
        compiler_params=pltpu.CompilerParams(
            collective_id=0, has_side_effects=True, vmem_limit_bytes=58 << 20
        ),
    )(
        tokens.T,
        ln1_gain,
        ln1_bias,
        qkv_weight.transpose(0, 2, 1),
        out_weight,
        ln2_gain,
        ln2_bias,
        merger_weight,
        group_segments,
        owners.reshape(1, -1),
    )


def solution(mesh):
    in_specs = (
        P("req", "tp"),
        P(),
        P(),
        P(None, None, "tp"),
        P("tp", None),
        P(),
        P(),
        P("req", "tp"),
        P("req", None),
        P("req", None),
    )
    out_specs = P("req", "tp")
    sizes = mesh.shape
    body = in_one_kernel if sizes["req"] == 8 and sizes["tp"] == 4 else local
    return jax.shard_map(body, mesh=mesh, in_specs=in_specs, out_specs=out_specs, check_vma=False)
```
